768 devices in a mesh: fsdp: 16 (over y, core), dp: 48 (over z, x).
Axes of the slice: x: 4, y: 8, z: 12, core: 2. Of those that a mesh axis runs over, the one named last changes fastest.
Arguments:
- gradients: float32 [48, 48, 512, 512], P('dp', None, 'fsdp'), may hold values from -0.625 to 0.625
- owners: int32 [48], replicated, may hold values from 0 to 15
- left_factor: float32 [48, 512, 512], P('dp', 'fsdp'), may hold values from -1 to 9, as said below
- right_factor: float32 [48, 512, 512], P('dp', 'fsdp'), may hold values from -1 to 9, as said below
- left_root: bfloat16 [48, 16, 512, 512], P('dp', 'fsdp'), may hold values from -1 to 3, as said below
- right_root: bfloat16 [48, 16, 512, 512], P('dp', 'fsdp'), may hold values from -1 to 3, as said below
Outputs:
- left_new: float32 [48, 512, 512], P('dp', 'fsdp')
- right_new: float32 [48, 512, 512], P('dp', 'fsdp')
- directions: bfloat16 [48, 512, 512], P('dp', 'fsdp')
The draws below stay inside these ranges and needn't reach their ends.
Inputs may be any that keep to these rules, and one draw needn't show every extreme that they name: `left_factor`: symmetric in its last two dimensions. `right_factor`: symmetric in its last two dimensions. `left_root`: symmetric in its last two dimensions. `right_root`: symmetric in its last two dimensions.
All inputs are finite; a program needn't handle non-finite values.
Results may differ from the reference program's by a relative error of at most 0.004.
Values may be sent and summed in bfloat16 or wider, within the bound.
No kernel may reach another device: no remote copies, remote signals or barrier semaphores. Data moves between devices by JAX's collectives and lax.ppermute only.
A program may use at most 32 MiB of HBM per device.

```python
import math
import jax
import jax.numpy as jnp
from jax import lax

BLK = 512
NB = 48
N_FSDP = 16
N_DP = 48


def symmetric_blocks(key, leading, lowest, highest, spread):
    noise_key, scale_key = jax.random.split(key)
    shape = leading + (BLK, BLK)
    noise = jax.random.truncated_normal(noise_key, -3.0, 3.0, shape, jnp.float32) * (spread / math.sqrt(BLK))
    noise = (noise + jnp.swapaxes(noise, -1, -2)) * 0.7071
    scales = jnp.exp(jax.random.uniform(scale_key, leading + (BLK,), jnp.float32, math.log(lowest), math.log(highest)))
    return noise + jnp.eye(BLK, dtype=jnp.float32) * scales[..., None, :]


def draw_left_factor(key, part):
    key = jax.random.fold_in(key, 11)
    return symmetric_blocks(key, (NB,), 1.0, 4.0, 0.3)


def draw_right_factor(key, part):
    key = jax.random.fold_in(key, 12)
    return symmetric_blocks(key, (NB,), 1.0, 4.0, 0.3)


def draw_left_root(key, part):
    key = jax.random.fold_in(key, 13)
    return symmetric_blocks(key, (NB, N_FSDP), 0.4, 1.5, 0.4).astype(jnp.bfloat16)


def draw_right_root(key, part):
    key = jax.random.fold_in(key, 14)
    return symmetric_blocks(key, (NB, N_FSDP), 0.4, 1.5, 0.4).astype(jnp.bfloat16)


def with_ends(result, rng, low, top_value):
    index_at = [jax.random.randint(jax.random.fold_in(rng, axis), (), 0, length) for axis, length in enumerate(result.shape)]
    longest = result.shape.index(max(result.shape))
    next_to = index_at[:longest] + [(index_at[longest] + 1) % result.shape[longest]] + index_at[longest + 1:]
    return result.at[tuple(index_at)].set(low).at[tuple(next_to)].set(top_value)


def spiked(array, key, source, target, parts, factor):
    def block_of(dim):
        return (jnp.arange(array.shape[dim]) // (array.shape[dim] // parts)).reshape((-1,) + (1,) * (array.ndim - 1 - dim))

    one_side = jax.random.permutation(key, parts)[block_of(target)]
    second = (block_of(target) + parts // 2) % parts
    return jnp.where((block_of(source) == one_side) | (block_of(source) == second), factor * array, array)


def levels(key, extent, cuts, low, largest):
    loudness, own = 1.0, jax.random.fold_in(key, 6)
    for dim, blocks in cuts:
        draws = jnp.exp(jax.random.uniform(jax.random.fold_in(own, dim), (blocks,), jnp.float32, low / len(cuts), largest / len(cuts)))
        loudness = loudness * jnp.repeat(draws, extent[dim] // blocks).reshape([-1 if axis == dim else 1 for axis in range(len(extent))])
    return loudness


def bell_draw_with(rng, shape, scale, bound, pieces, heavy, kind=jnp.bfloat16):
    entries = scale * jax.random.normal(rng, shape, jnp.float32)
    if pieces:
        entries = entries * levels(rng, shape, pieces, -0.22, 0.18)
    return jnp.clip(spiked(entries, jax.random.fold_in(rng, 3), *heavy), -bound, bound).astype(kind)


def setup_inputs(seed: int = 0) -> dict:
    seeds = jax.random.split(jax.random.key(seed), 7)
    gradients = bell_draw_with(seeds[0], (N_DP, NB, BLK, BLK), 0.02, 0.625, ((0, 48), (2, 16)), (0, 1, 48, 3.25), jnp.float32)
    owners = with_ends(jax.random.randint(seeds[1], (NB,), 0, N_FSDP), jax.random.fold_in(seeds[1], 1), 0, N_FSDP - 1).astype(jnp.int32)
    left_factor = draw_left_factor(jax.random.fold_in(seeds[6], 71), 0)
    right_factor = draw_right_factor(jax.random.fold_in(seeds[6], 71), 0)
    left_root = draw_left_root(jax.random.fold_in(seeds[6], 71), 0)
    right_root = draw_right_root(jax.random.fold_in(seeds[6], 71), 0)
    return dict(gradients=gradients, owners=owners, left_factor=left_factor, right_factor=right_factor, left_root=left_root, right_root=right_root)


def block_step(items):
    block, left_old, right_old, left_inverse, right_inverse = items
    left_stat = lax.dot_general(block, block, (((1,), (1,)), ((), ())), precision=lax.Precision.HIGHEST)
    right_stat = lax.dot_general(block, block, (((0,), (0,)), ((), ())), precision=lax.Precision.HIGHEST)
    product = jnp.dot(left_inverse.astype(jnp.float32), block, precision=lax.Precision.HIGHEST)
    product = jnp.dot(product, right_inverse.astype(jnp.float32), precision=lax.Precision.HIGHEST)
    return (0.9 * left_old + 0.1 * left_stat, 0.9 * right_old + 0.1 * right_stat, product.astype(jnp.bfloat16))


def reference(gradients, owners, left_factor, right_factor, left_root, right_root):
    summed = jnp.sum(gradients, axis=0)
    indices = jnp.arange(NB, dtype=jnp.int32)
    left_pick = left_root[indices, owners]
    right_pick = right_root[indices, owners]
    left_new, right_new, directions = lax.map(block_step, (summed, left_factor, right_factor, left_pick, right_pick))
    return left_new, right_new, directions
```

```python
import jax
import jax.numpy as jnp
from jax import lax
from jax.sharding import Mesh
from jax.sharding import PartitionSpec as P

Y, C, Z, X = 8, 2, 12, 4
BF, F32 = jnp.bfloat16, jnp.float32
ROWS = ("y", "c")


def to_column(value, step):
    return lax.ppermute(value, "x", [(i, (i + step) % X) for i in range(X)])


def mm(a, b, ca, cb):
    return lax.dot_general(a, b, (((ca,), (cb,)), ((), ())), preferred_element_type=F32)


def on_device(gradients, owners, left_factor, right_factor, left_root, right_root):
    rows, width = gradients.shape[2:]
    mine = gradients.reshape(Z, X, rows, width)
    x, z = lax.axis_index("x"), lax.axis_index("z")
    me = lax.axis_index("y") * C + lax.axis_index("c")

    def column(step):
        return lax.dynamic_index_in_dim(mine, lax.rem(x + step, X), 1, keepdims=False)

    with jax.named_scope("sum_over_x"):
        came = [to_column(column(step).astype(BF), step) for step in (2, 1, 3)]
        partial = column(0) + came[0].astype(F32) + came[1].astype(F32) + came[2].astype(F32)
    with jax.named_scope("sum_over_z"):
        got = lax.all_to_all(partial.astype(BF), "z", 0, 0, tiled=True)
        my_rows = jnp.sum(got.astype(F32), axis=0).astype(BF)
    with jax.named_scope("whole_block"):
        whole = lax.all_gather(my_rows, ROWS, axis=0, tiled=True)
    with jax.named_scope("direction"):
        left = mm(left_root[0, 0], whole, 1, 0)
        high = left.astype(BF)
        low = (left - high.astype(F32)).astype(BF)
        product = (mm(high, right_root[0, 0], 1, 0) + mm(low, right_root[0, 0], 1, 0)).astype(BF)
        every = lax.all_to_all(product.reshape(Y * C, rows, width), ROWS, 0, 0, tiled=True)
        directions = lax.dynamic_index_in_dim(every, owners[z * X + x], 0, keepdims=True)
    with jax.named_scope("statistics"):
        columns = lax.dynamic_slice_in_dim(whole, me * rows, rows, 1)
        left_new = 0.9 * left_factor + 0.1 * mm(my_rows, whole, 1, 1)[None]
        right_new = 0.9 * right_factor + 0.1 * mm(columns, whole, 0, 0)[None]
    return left_new, right_new, directions


def solution(mesh):
    grid = Mesh(mesh.devices.reshape(Y, C, Z, X), ("y", "c", "z", "x"))
    dp = ("z", "x")
    stat = P(dp, ROWS, None)
    return jax.shard_map(
        on_device,
        mesh=grid,
        in_specs=(P(dp, None, ROWS, None), P(), stat, stat, P(dp, ROWS, None, None), P(dp, ROWS, None, None)),
        out_specs=(stat, stat, stat),
        check_vma=False,
    )
```

```python
import jax
import jax.numpy as jnp
from jax import lax
from jax.sharding import Mesh
from jax.sharding import PartitionSpec as P

Y, C, Z, X = 8, 2, 12, 4
ZN = 3
ZF = Z // ZN
BF, F32 = jnp.bfloat16, jnp.float32
ROWS = ("y", "c")


def along_x(value, step):
    return lax.ppermute(value, "x", [(i, (i + step) % X) for i in range(X)])


def near_z(value, step):
    return lax.ppermute(value, "z", [(i, i - i % ZN + (i + step) % ZN) for i in range(Z)])


def far_z(value, step):
    return lax.ppermute(value, "z", [(i, (i + step * ZN) % Z) for i in range(Z)])


def mm(a, b, ca, cb):
    return lax.dot_general(a, b, (((ca,), (cb,)), ((), ())), preferred_element_type=F32)


def pick(array, index, axis):
    return lax.dynamic_index_in_dim(array, index, axis, keepdims=False)


def on_device(gradients, owners, left_factor, right_factor, left_root, right_root):
    rows, width = gradients.shape[2:]
    mine = gradients.reshape(Z, X, rows, width)
    x, z = lax.axis_index("x"), lax.axis_index("z")
    near, far = lax.rem(z, ZN), lax.div(z, ZN)
    me = lax.axis_index("y") * C + lax.axis_index("c")

    with jax.named_scope("sum_over_x"):
        to_x = [pick(mine, lax.rem(x + step, X), 1).astype(BF) for step in (2, 1, 3)]
        came = [along_x(v, step).reshape(ZF, ZN, rows, width) for v, step in zip(to_x, (2, 1, 3))]
    with jax.named_scope("owner_roots"):
        owner, core = owners[z * X + x], lax.axis_index("c")
        here = lax.rem(owner, C) == core
        left_root, right_root = left_root[0, 0], right_root[0, 0]
        left_inverse = jnp.where(here, left_root, lax.ppermute(left_root, "c", [(0, 1), (1, 0)]))
        right_inverse = jnp.where(here, right_root, lax.ppermute(right_root, "c", [(0, 1), (1, 0)]))
        left_inverse = pick(left_inverse.reshape(Y, C, rows, width), core, 1).reshape(-1, width)
    with jax.named_scope("sum_over_near_z"):
        kept = pick(mine, x, 1).reshape(ZF, ZN, rows, width)

        def over_x(step):
            at = lax.rem(near + step, ZN)
            return sum((pick(v, at, 1).astype(F32) for v in came), pick(kept, at, 1))

        came_z = [near_z(over_x(step).astype(BF), step) for step in (2, 1)]
        over_near = over_x(0)
    with jax.named_scope("sum_over_far_z"):

        def over_z(step):
            at = lax.rem(far + step, ZF)
            return sum((pick(v, at, 0).astype(F32) for v in came_z), pick(over_near, at, 0))

        came_far = [far_z(over_z(step).astype(BF), step) for step in (2, 1, 3)]
        my_rows = sum((v.astype(F32) for v in came_far), over_z(0)).astype(BF)
    with jax.named_scope("whole_block"):
        whole = lax.all_gather(my_rows, ROWS, axis=0, tiled=True)
    with jax.named_scope("direction"):
        left = mm(left_inverse, whole, 1, 0)
        high = lax.reduce_precision(left, 8, 7)
        low = (left - high).astype(BF)
        product = (mm(high.astype(BF), right_inverse, 1, 0) + mm(low, right_inverse, 1, 0)).astype(BF)
        every = lax.all_to_all(product.reshape(Y, rows, width), "y", 0, 0, tiled=True)
        directions = lax.dynamic_index_in_dim(every, lax.div(owner, C), 0, keepdims=True)
    with jax.named_scope("statistics"):
        columns = lax.dynamic_slice_in_dim(whole, me * rows, rows, 1)
        left_new = 0.9 * left_factor + 0.1 * mm(my_rows, whole, 1, 1)[None]
        right_new = 0.9 * right_factor + 0.1 * mm(columns, whole, 0, 0)[None]
    return left_new, right_new, directions


def solution(mesh):
    grid = Mesh(mesh.devices.reshape(Y, C, Z, X), ("y", "c", "z", "x"))
    dp = ("z", "x")
    stat = P(dp, ROWS, None)
    return jax.shard_map(
        on_device,
        mesh=grid,
        in_specs=(P(dp, None, ROWS, None), P(), stat, stat, P(dp, ROWS, None, None), P(dp, ROWS, None, None)),
        out_specs=(stat, stat, stat),
        check_vma=False,
    )
```

```python
import jax
import jax.numpy as jnp
from jax import lax
from jax.sharding import Mesh
from jax.sharding import PartitionSpec as P

Y, C, Z, X = 8, 2, 12, 4
BF, F32 = jnp.bfloat16, jnp.float32
ROWS = ("y", "c")


def mm(a, b, ca, cb):
    return lax.dot_general(a, b, (((ca,), (cb,)), ((), ())), preferred_element_type=F32)


def pick(array, index, axis):
    return lax.dynamic_index_in_dim(array, index, axis, keepdims=False)


def added(parts):
    total = parts[0].astype(F32)
    for i in range(1, parts.shape[0]):
        total = total + parts[i].astype(F32)
    return total


def on_device(gradients, owners, left_factor, right_factor, left_root, right_root):
    rows, width = gradients.shape[2:]
    x, z = lax.axis_index("x"), lax.axis_index("z")
    me = lax.axis_index("y") * C + lax.axis_index("c")

    with jax.named_scope("sum_over_x"):
        by_x = gradients.reshape(Z, X, rows, width).astype(BF).transpose(1, 0, 2, 3)
        over_x = added(lax.all_to_all(by_x, "x", 0, 0, tiled=True))
    with jax.named_scope("owner_roots"):
        owner, core = owners[z * X + x], lax.axis_index("c")
        here = lax.rem(owner, C) == core
        left_root, right_root = left_root[0, 0], right_root[0, 0]
        left_inverse = jnp.where(here, left_root, lax.ppermute(left_root, "c", [(0, 1), (1, 0)]))
        right_inverse = jnp.where(here, right_root, lax.ppermute(right_root, "c", [(0, 1), (1, 0)]))
        left_inverse = pick(left_inverse.reshape(Y, C, rows, width), core, 1).reshape(-1, width)
    with jax.named_scope("sum_over_z"):
        my_rows = added(lax.all_to_all(over_x.astype(BF), "z", 0, 0, tiled=True)).astype(BF)
    with jax.named_scope("whole_block"):
        whole = lax.all_gather(my_rows, ROWS, axis=0, tiled=True)
    with jax.named_scope("direction"):
        left = mm(left_inverse, whole, 1, 0)
        high = lax.reduce_precision(left, 8, 7)
        low = (left - high).astype(BF)
        product = (mm(high.astype(BF), right_inverse, 1, 0) + mm(low, right_inverse, 1, 0)).astype(BF)
        every = lax.all_to_all(product.reshape(Y, rows, width), "y", 0, 0, tiled=True)
        directions = lax.dynamic_index_in_dim(every, lax.div(owner, C), 0, keepdims=True)
    with jax.named_scope("statistics"):
        columns = lax.dynamic_slice_in_dim(whole, me * rows, rows, 1)
        left_new = 0.9 * left_factor + 0.1 * mm(my_rows, whole, 1, 1)[None]
        right_new = 0.9 * right_factor + 0.1 * mm(columns, whole, 0, 0)[None]
    return left_new, right_new, directions


def solution(mesh):
    grid = Mesh(mesh.devices.reshape(Y, C, Z, X), ("y", "c", "z", "x"))
    dp = ("z", "x")
    stat = P(dp, ROWS, None)
    return jax.shard_map(
        on_device,
        mesh=grid,
        in_specs=(P(dp, None, ROWS, None), P(), stat, stat, P(dp, ROWS, None, None), P(dp, ROWS, None, None)),
        out_specs=(stat, stat, stat),
        check_vma=False,
    )
```

```python
import jax
import jax.numpy as jnp
from jax import lax
from jax.sharding import Mesh
from jax.sharding import PartitionSpec as P

Y, C, Z, X = 8, 2, 12, 4
BF, F32 = jnp.bfloat16, jnp.float32
ROWS = ("y", "c")


def along_x(value, step):
    return lax.ppermute(value, "x", [(i, (i + step) % X) for i in range(X)])


def mm(a, b, ca, cb):
    return lax.dot_general(a, b, (((ca,), (cb,)), ((), ())), preferred_element_type=F32)


def pick(array, index, axis):
    return lax.dynamic_index_in_dim(array, index, axis, keepdims=False)


def added(parts):
    total = parts[0].astype(F32)
    for i in range(1, parts.shape[0]):
        total = total + parts[i].astype(F32)
    return total


def on_device(gradients, owners, left_factor, right_factor, left_root, right_root):
    rows, width = gradients.shape[2:]
    x, z = lax.axis_index("x"), lax.axis_index("z")
    me = lax.axis_index("y") * C + lax.axis_index("c")

    mine = gradients.reshape(Z, X, rows, width)

    def column(step):
        return pick(mine, lax.rem(x + step, X), 1)

    with jax.named_scope("sum_over_x"):
        came = [along_x(column(step).astype(BF), step) for step in (2, 1, 3)]
        over_x = sum((v.astype(F32) for v in came), column(0))
    with jax.named_scope("owner_roots"):
        slots = jnp.concatenate(
            [left_root.reshape(Y * C, rows, width), right_root.reshape(Y * C, rows, width)], axis=1
        )
        roots = pick(lax.all_to_all(slots, ROWS, 0, 0, tiled=True), owners[z * X + x], 0)
        over_x, roots = lax.optimization_barrier((over_x.astype(BF), roots))
        right_inverse = lax.all_gather(roots[rows:], ROWS, axis=0, tiled=True)
    with jax.named_scope("sum_over_z"):
        exact = added(lax.all_to_all(over_x, "z", 0, 0, tiled=True))
        my_rows = exact.astype(BF)
    with jax.named_scope("whole_block"):
        my_rows, right_inverse = lax.optimization_barrier((my_rows, right_inverse))
        whole = lax.all_gather(my_rows, ROWS, axis=0, tiled=True)
    with jax.named_scope("direction"):
        rest = (exact - lax.reduce_precision(exact, 8, 7)).astype(BF)
        corner = lax.dynamic_slice_in_dim(roots[:rows], me * rows, rows, 1)
        left = mm(roots[:rows], whole, 1, 0) + mm(corner, rest, 1, 0)
        high = lax.reduce_precision(left, 8, 7)
        low = (left - high).astype(BF)
        product = mm(high.astype(BF), right_inverse, 1, 0) + mm(low, right_inverse, 1, 0)
        directions = product.astype(BF)[None]
    with jax.named_scope("statistics"):
        columns = lax.dynamic_slice_in_dim(whole, me * rows, rows, 1)
        left_new = 0.9 * left_factor + 0.1 * mm(my_rows, whole, 1, 1)[None]
        right_new = 0.9 * right_factor + 0.1 * mm(columns, whole, 0, 0)[None]
    return left_new, right_new, directions


def solution(mesh):
    grid = Mesh(mesh.devices.reshape(Y, C, Z, X), ("y", "c", "z", "x"))
    dp = ("z", "x")
    stat = P(dp, ROWS, None)
    return jax.shard_map(
        on_device,
        mesh=grid,
        in_specs=(P(dp, None, ROWS, None), P(), stat, stat, P(dp, ROWS, None, None), P(dp, ROWS, None, None)),
        out_specs=(stat, stat, stat),
        check_vma=False,
    )
```

```python
import jax
import jax.numpy as jnp
from jax import lax
from jax.experimental import pallas as pl
from jax.experimental.pallas import tpu as pltpu
from jax.sharding import Mesh
from jax.sharding import PartitionSpec as P

Y, C, Z, X = 8, 2, 12, 4
BF, F32 = jnp.bfloat16, jnp.float32
ROWS = ("y", "c")


def along_x(value, step):
    return lax.ppermute(value, "x", [(i, (i + step) % X) for i in range(X)])


def mm(a, b, ca, cb):
    return lax.dot_general(a, b, (((ca,), (cb,)), ((), ())), preferred_element_type=F32)


def pick(array, index, axis):
    return lax.dynamic_index_in_dim(array, index, axis, keepdims=False)


def added(parts):
    total = parts[0].astype(F32)
    for i in range(1, parts.shape[0]):
        total = total + parts[i].astype(F32)
    return total


def stacked(left, right):
    count, rows, width = left.shape
    half = count // 2

    def kernel(left_ref, right_ref, out_ref, sems):
        copies = []
        for i in range(2):
            part = pl.ds(i * half, half)
            for j, ref in enumerate((left_ref, right_ref)):
                to = out_ref.at[part, pl.ds(j * rows, rows)]
                copies.append(pltpu.make_async_copy(ref.at[part], to, sems.at[2 * i + j]))
        for copy in copies:
            copy.start()
        for copy in copies:
            copy.wait()

    return pl.pallas_call(
        kernel,
        out_shape=jax.ShapeDtypeStruct((count, 2 * rows, width), left.dtype),
        in_specs=[pl.BlockSpec(memory_space=pl.ANY)] * 2,
        out_specs=pl.BlockSpec(memory_space=pl.ANY),
        scratch_shapes=[pltpu.SemaphoreType.DMA((4,))],
        cost_estimate=pl.CostEstimate(flops=0, bytes_accessed=4 * left.size * 2, transcendentals=0),
    )(left, right)


def after_gather(me, whole, right_inverse, left_rows, exact, left_factor, right_factor):
    rows, width = exact.shape
    slab = 128 // rows

    def kernel(me_ref, whole_ref, right_ref, lrows_ref, exact_ref, lf_ref, rf_ref, ln_ref, rn_ref, d_ref, rest, stat):
        me = me_ref[0]
        first = pl.multiple_of((me // slab) * 128, 128)
        mine = pl.multiple_of((me % slab) * rows, rows)
        block = whole_ref[...]
        exact = exact_ref[...]
        my_rows = exact.astype(BF)
        rest[...] = jnp.zeros_like(rest)
        rest[pl.ds(mine, rows), :] = (exact - my_rows.astype(F32)).astype(BF)
        left = mm(lrows_ref[...], block, 1, 0) + mm(lrows_ref[:, pl.ds(first, 128)], rest[...], 1, 0)
        high = left.astype(BF)
        low = (left - high.astype(F32)).astype(BF)
        right = right_ref[...]
        d_ref[0] = (mm(high, right, 1, 0) + mm(low, right, 1, 0)).astype(BF)
        ln_ref[...] = 0.9 * lf_ref[...] + 0.1 * mm(my_rows, block, 1, 1)[None]
        stat[...] = mm(whole_ref[:, pl.ds(first, 128)], block, 0, 0)
        rn_ref[...] = 0.9 * rf_ref[...] + 0.1 * stat[pl.ds(mine, rows), :][None]

    vmem = pl.BlockSpec(memory_space=pltpu.VMEM)
    stat_shape = jax.ShapeDtypeStruct((1, rows, width), F32)
    return pl.pallas_call(
        kernel,
        out_shape=(stat_shape, stat_shape, jax.ShapeDtypeStruct((1, rows, width), BF)),
        in_specs=[pl.BlockSpec(memory_space=pltpu.SMEM)] + [vmem] * 6,
        out_specs=(vmem, vmem, vmem),
        scratch_shapes=[pltpu.VMEM((128, width), BF), pltpu.VMEM((128, width), F32)],
        cost_estimate=pl.CostEstimate(flops=10**8, bytes_accessed=2 << 20, transcendentals=0),
    )(me, whole, right_inverse, left_rows, exact, left_factor, right_factor)


def x_sum(x, gradients, came):
    parts, _, rows, width = gradients.shape
    step = 4

    def kernel(x_ref, own_ref, a_ref, b_ref, c_ref, out_ref):
        total = own_ref[:, 0] + a_ref[...].astype(F32) + b_ref[...].astype(F32) + c_ref[...].astype(F32)
        out_ref[...] = total.astype(BF)

    part = pl.BlockSpec((step, rows, width), lambda i, x_ref: (i, 0, 0))
    own = pl.BlockSpec((step, 1, rows, width), lambda i, x_ref: (i, x_ref[0], 0, 0))
    return pl.pallas_call(
        kernel,
        out_shape=jax.ShapeDtypeStruct((parts, rows, width), BF),
        grid_spec=pltpu.PrefetchScalarGridSpec(
            num_scalar_prefetch=1, grid=(parts // step,), in_specs=[own, part, part, part], out_specs=part
        ),
        cost_estimate=pl.CostEstimate(flops=10**6, bytes_accessed=3 << 20, transcendentals=0),
    )(x, gradients, *came)


def on_device(gradients, owners, left_factor, right_factor, left_root, right_root):
    rows, width = gradients.shape[2:]
    x, z = lax.axis_index("x"), lax.axis_index("z")
    me = lax.axis_index("y") * C + lax.axis_index("c")
    mine = gradients.reshape(Z, X, rows, width)

    def column(step):
        return pick(mine, lax.rem(x + step, X), 1)

    with jax.named_scope("sum_over_x"):
        came = [along_x(column(step).astype(BF), step) for step in (2, 1, 3)]
        over_x = x_sum(x[None], mine, came)
    with jax.named_scope("owner_roots"):
        slots = stacked(left_root.reshape(Y * C, rows, width), right_root.reshape(Y * C, rows, width))
        roots = pick(lax.all_to_all(slots, ROWS, 0, 0, tiled=True), owners[z * X + x], 0)
        over_x, roots = lax.optimization_barrier((over_x, roots))
        right_inverse = lax.all_gather(roots[rows:], ROWS, axis=0, tiled=True)
    with jax.named_scope("sum_over_z"):
        exact = added(lax.all_to_all(over_x, "z", 0, 0, tiled=True))
        my_rows = exact.astype(BF)
    with jax.named_scope("whole_block"):
        my_rows, right_inverse = lax.optimization_barrier((my_rows, right_inverse))
        whole = lax.all_gather(my_rows, ROWS, axis=0, tiled=True)
    with jax.named_scope("direction_and_statistics"):
        return after_gather(me[None], whole, right_inverse, roots[:rows], exact, left_factor, right_factor)


def solution(mesh):
    grid = Mesh(mesh.devices.reshape(Y, C, Z, X), ("y", "c", "z", "x"))
    dp = ("z", "x")
    stat = P(dp, ROWS, None)
    return jax.shard_map(
        on_device,
        mesh=grid,
        in_specs=(P(dp, None, ROWS, None), P(), stat, stat, P(dp, ROWS, None, None), P(dp, ROWS, None, None)),
        out_specs=(stat, stat, stat),
        check_vma=False,
    )
```

```python
import jax
import jax.numpy as jnp
from jax import lax
from jax.experimental import pallas as pl
from jax.experimental.pallas import tpu as pltpu
from jax.sharding import Mesh
from jax.sharding import PartitionSpec as P

Y, C, Z, X = 8, 2, 12, 4
BF, F32 = jnp.bfloat16, jnp.float32
ROWS = ("y", "c")


def along_x(value, step):
    return lax.ppermute(value, "x", [(i, (i + step) % X) for i in range(X)])


def mm(a, b, ca, cb):
    return lax.dot_general(a, b, (((ca,), (cb,)), ((), ())), preferred_element_type=F32)


def pick(array, index, axis):
    return lax.dynamic_index_in_dim(array, index, axis, keepdims=False)


def added(parts):
    total = parts[0].astype(F32)
    for i in range(1, parts.shape[0]):
        total = total + parts[i].astype(F32)
    return total


def in_vmem(value):
    return pltpu.with_memory_space_constraint(value, pltpu.VMEM)


SMEM, VMEM = pl.BlockSpec(memory_space=pltpu.SMEM), pl.BlockSpec(memory_space=pltpu.VMEM)


def cost(flops, size):
    return pl.CostEstimate(flops=flops, bytes_accessed=size, transcendentals=0)


def rows_to_send(where, left, right, other_left, other_right):
    _, _, rows, width = left.shape

    def kernel(where_ref, left_ref, right_ref, other_left_ref, other_right_ref, out_ref):
        core = where_ref[1]

        @pl.when(where_ref[0] == 1)
        def _():
            out_ref[:, :rows] = left_ref[:, core]
            out_ref[:, rows:] = right_ref[:, core]

        @pl.when(where_ref[0] == 0)
        def _():
            out_ref[:, :rows] = other_left_ref[:, core]
            out_ref[:, rows:] = other_right_ref[:, core]

    return pl.pallas_call(
        kernel,
        out_shape=pltpu.VMEM((Y, 2 * rows, width), BF),
        in_specs=[SMEM] + [VMEM] * 4,
        out_specs=VMEM,
        cost_estimate=cost(10**6, 1 << 20),
    )(where, *(in_vmem(v) for v in (left, right, other_left, other_right)))


def x_sum(own, came):
    def kernel(own_ref, a_ref, b_ref, c_ref, out_ref):
        for i in range(own_ref.shape[0]):
            total = own_ref[i] + a_ref[i].astype(F32) + b_ref[i].astype(F32) + c_ref[i].astype(F32)
            out_ref[i] = total.astype(BF)

    return pl.pallas_call(
        kernel,
        out_shape=pltpu.VMEM(own.shape, BF),
        in_specs=[VMEM] * 4,
        out_specs=VMEM,
        cost_estimate=cost(5 * 10**10, 2 << 20),
    )(*(in_vmem(v) for v in (own, *came)))


def after_gather(me, whole, right_inverse, left_rows, exact, left_factor, right_factor):
    rows, width = exact.shape
    slab = 128 // rows

    def kernel(me_ref, whole_ref, right_ref, lrows_ref, exact_ref, lf_ref, rf_ref, ln_ref, rn_ref, d_ref, rest, stat):
        me = me_ref[0]
        first = pl.multiple_of((me // slab) * 128, 128)
        mine = pl.multiple_of((me % slab) * rows, rows)
        block = whole_ref[...]
        exact = exact_ref[...]
        my_rows = exact.astype(BF)
        rest[...] = jnp.zeros_like(rest)
        rest[pl.ds(mine, rows), :] = (exact - my_rows.astype(F32)).astype(BF)
        left = mm(lrows_ref[...], block, 1, 0) + mm(lrows_ref[:, pl.ds(first, 128)], rest[...], 1, 0)
        high = left.astype(BF)
        low = (left - high.astype(F32)).astype(BF)
        right = right_ref[...]
        d_ref[0] = (mm(high, right, 1, 0) + mm(low, right, 1, 0)).astype(BF)
        ln_ref[...] = 0.9 * lf_ref[...] + 0.1 * mm(my_rows, block, 1, 1)[None]
        stat[...] = mm(whole_ref[:, pl.ds(first, 128)], block, 0, 0)
        rn_ref[...] = 0.9 * rf_ref[...] + 0.1 * stat[pl.ds(mine, rows), :][None]

    stat_shape = jax.ShapeDtypeStruct((1, rows, width), F32)
    return pl.pallas_call(
        kernel,
        out_shape=(stat_shape, stat_shape, jax.ShapeDtypeStruct((1, rows, width), BF)),
        in_specs=[SMEM] + [VMEM] * 6,
        out_specs=(VMEM, VMEM, VMEM),
        scratch_shapes=[pltpu.VMEM((128, width), BF), pltpu.VMEM((128, width), F32)],
        cost_estimate=cost(10**8, 2 << 20),
    )(me, *(in_vmem(v) for v in (whole, right_inverse, left_rows, exact, left_factor, right_factor)))


def on_device(gradients, owners, left_factor, right_factor, left_root, right_root):
    rows, width = gradients.shape[2:]
    x, z, core = lax.axis_index("x"), lax.axis_index("z"), lax.axis_index("c")
    me = lax.axis_index("y") * C + core
    mine = gradients.reshape(Z, X, rows, width)
    owner = owners[z * X + x]

    def column(step):
        return pick(mine, lax.rem(x + step, X), 1)

    with jax.named_scope("sum_over_x"):
        to_x = [column(step).astype(BF) for step in (2, 1, 3)]
        came = [along_x(v, step) for v, step in zip(to_x, (2, 1, 3))]
        over_x = x_sum(column(0), came)
    with jax.named_scope("owner_roots"):
        pair = [root.reshape(Y, C, rows, width) for root in (left_root, right_root)]
        others = [lax.ppermute(root.reshape(-1, width), "c", [(0, 1), (1, 0)]) for root in pair]
        where = jnp.stack([(lax.rem(owner, C) == core).astype(jnp.int32), core])
        slots = rows_to_send(where, *pair, *(v.reshape(pair[0].shape) for v in others))
        roots = pick(lax.all_to_all(slots, "y", 0, 0, tiled=True), lax.div(owner, C), 0)
        over_x, roots = lax.optimization_barrier((over_x, roots))
        right_inverse = lax.all_gather(roots[rows:], ROWS, axis=0, tiled=True)
    with jax.named_scope("sum_over_z"):
        exact = added(lax.all_to_all(over_x, "z", 0, 0, tiled=True))
        my_rows = exact.astype(BF)
    with jax.named_scope("whole_block"):
        my_rows, right_inverse = lax.optimization_barrier((my_rows, right_inverse))
        whole = lax.all_gather(my_rows, ROWS, axis=0, tiled=True)
    with jax.named_scope("direction_and_statistics"):
        return after_gather(me[None], whole, right_inverse, roots[:rows], exact, left_factor, right_factor)


def solution(mesh):
    grid = Mesh(mesh.devices.reshape(Y, C, Z, X), ("y", "c", "z", "x"))
    dp = ("z", "x")
    stat = P(dp, ROWS, None)
    return jax.shard_map(
        on_device,
        mesh=grid,
        in_specs=(P(dp, None, ROWS, None), P(), stat, stat, P(dp, ROWS, None, None), P(dp, ROWS, None, None)),
        out_specs=(stat, stat, stat),
        check_vma=False,
    )
```

```python
import jax
import jax.numpy as jnp
from jax import lax
from jax.experimental import pallas as pl
from jax.experimental.pallas import tpu as pltpu
from jax.sharding import Mesh
from jax.sharding import PartitionSpec as P

Y, C, Z, X = 8, 2, 12, 4
BF, F32 = jnp.bfloat16, jnp.float32
ROWS = ("y", "c")


def along_x(value, step):
    return lax.ppermute(value, "x", [(i, (i + step) % X) for i in range(X)])


def mm(a, b, ca, cb):
    return lax.dot_general(a, b, (((ca,), (cb,)), ((), ())), preferred_element_type=F32)


def pick(array, index, axis):
    return lax.dynamic_index_in_dim(array, index, axis, keepdims=False)


def added(parts):
    total = parts[0].astype(F32)
    for i in range(1, parts.shape[0]):
        total = total + parts[i].astype(F32)
    return total


def in_vmem(value):
    return pltpu.with_memory_space_constraint(value, pltpu.VMEM)


SMEM, VMEM = pl.BlockSpec(memory_space=pltpu.SMEM), pl.BlockSpec(memory_space=pltpu.VMEM)


def cost(flops, size):
    return pl.CostEstimate(flops=flops, bytes_accessed=size, transcendentals=0)


def stacked(left, right):
    count, rows, width = left.shape

    def kernel(left_ref, right_ref, out_ref):
        out_ref[:, :rows] = left_ref[...]
        out_ref[:, rows:] = right_ref[...]

    return pl.pallas_call(
        kernel,
        out_shape=jax.ShapeDtypeStruct((count, 2 * rows, width), BF),
        in_specs=[VMEM] * 2,
        out_specs=VMEM,
        cost_estimate=cost(10**6, 1 << 20),
    )(in_vmem(left), in_vmem(right))


def after_gather(me, whole, right_inverse, left_rows, exact, left_factor, right_factor):
    rows, width = exact.shape
    slab = 128 // rows

    def kernel(me_ref, whole_ref, right_ref, lrows_ref, exact_ref, lf_ref, rf_ref, ln_ref, rn_ref, d_ref, rest, stat):
        me = me_ref[0]
        first = pl.multiple_of((me // slab) * 128, 128)
        mine = pl.multiple_of((me % slab) * rows, rows)
        block = whole_ref[...]
        exact = exact_ref[...]
        my_rows = exact.astype(BF)
        rest[...] = jnp.zeros_like(rest)
        rest[pl.ds(mine, rows), :] = (exact - my_rows.astype(F32)).astype(BF)
        left = mm(lrows_ref[...], block, 1, 0) + mm(lrows_ref[:, pl.ds(first, 128)], rest[...], 1, 0)
        high = left.astype(BF)
        low = (left - high.astype(F32)).astype(BF)
        right = right_ref[...]
        d_ref[0] = (mm(high, right, 1, 0) + mm(low, right, 1, 0)).astype(BF)
        ln_ref[...] = 0.9 * lf_ref[...] + 0.1 * mm(my_rows, block, 1, 1)[None]
        stat[...] = mm(whole_ref[:, pl.ds(first, 128)], block, 0, 0)
        rn_ref[...] = 0.9 * rf_ref[...] + 0.1 * stat[pl.ds(mine, rows), :][None]

    stat_shape = jax.ShapeDtypeStruct((1, rows, width), F32)
    return pl.pallas_call(
        kernel,
        out_shape=(stat_shape, stat_shape, jax.ShapeDtypeStruct((1, rows, width), BF)),
        in_specs=[SMEM] + [VMEM] * 6,
        out_specs=(VMEM, VMEM, VMEM),
        scratch_shapes=[pltpu.VMEM((128, width), BF), pltpu.VMEM((128, width), F32)],
        cost_estimate=cost(10**8, 2 << 20),
    )(me, *(in_vmem(v) for v in (whole, right_inverse, left_rows, exact, left_factor, right_factor)))


def on_device(gradients, owners, left_factor, right_factor, left_root, right_root):
    rows, width = gradients.shape[2:]
    x, z = lax.axis_index("x"), lax.axis_index("z")
    me = lax.axis_index("y") * C + lax.axis_index("c")

    mine = gradients.reshape(Z, X, rows, width)

    def column(step):
        return pick(mine, lax.rem(x + step, X), 1)

    with jax.named_scope("sum_over_x"):
        came = [along_x(column(step).astype(BF), step) for step in (2, 1, 3)]
        over_x = sum((v.astype(F32) for v in came), column(0))
    with jax.named_scope("owner_roots"):
        slots = stacked(left_root.reshape(Y * C, rows, width), right_root.reshape(Y * C, rows, width))
        roots = pick(lax.all_to_all(slots, ROWS, 0, 0, tiled=True), owners[z * X + x], 0)
        over_x, roots = lax.optimization_barrier((over_x.astype(BF), roots))
        right_inverse = lax.all_gather(roots[rows:], ROWS, axis=0, tiled=True)
    with jax.named_scope("sum_over_z"):
        exact = added(lax.all_to_all(over_x, "z", 0, 0, tiled=True))
        my_rows = exact.astype(BF)
    with jax.named_scope("whole_block"):
        my_rows, right_inverse = lax.optimization_barrier((my_rows, right_inverse))
        whole = lax.all_gather(my_rows, ROWS, axis=0, tiled=True)
    with jax.named_scope("direction_and_statistics"):
        return after_gather(me[None], whole, right_inverse, roots[:rows], exact, left_factor, right_factor)


def solution(mesh):
    grid = Mesh(mesh.devices.reshape(Y, C, Z, X), ("y", "c", "z", "x"))
    dp = ("z", "x")
    stat = P(dp, ROWS, None)
    return jax.shard_map(
        on_device,
        mesh=grid,
        in_specs=(P(dp, None, ROWS, None), P(), stat, stat, P(dp, ROWS, None, None), P(dp, ROWS, None, None)),
        out_specs=(stat, stat, stat),
        check_vma=False,
    )
```

```python
import jax
import jax.numpy as jnp
from jax import lax
from jax.experimental import pallas as pl
from jax.experimental.pallas import tpu as pltpu
from jax.sharding import Mesh
from jax.sharding import PartitionSpec as P

Y, C, Z, X = 8, 2, 12, 4
BF, F32 = jnp.bfloat16, jnp.float32
ROWS = ("y", "c")


def along_x(value, step):
    return lax.ppermute(value, "x", [(i, (i + step) % X) for i in range(X)])


def mm(a, b, ca, cb):
    return lax.dot_general(a, b, (((ca,), (cb,)), ((), ())), preferred_element_type=F32)


def pick(array, index, axis):
    return lax.dynamic_index_in_dim(array, index, axis, keepdims=False)


def added(parts):
    total = parts[0].astype(F32)
    for i in range(1, parts.shape[0]):
        total = total + parts[i].astype(F32)
    return total


def in_vmem(value):
    return pltpu.with_memory_space_constraint(value, pltpu.VMEM)


SMEM, VMEM = pl.BlockSpec(memory_space=pltpu.SMEM), pl.BlockSpec(memory_space=pltpu.VMEM)


def cost(flops, size):
    return pl.CostEstimate(flops=flops, bytes_accessed=size, transcendentals=0)


def stacked(left, right):
    count, rows, width = left.shape
    shape = (count, 2 * rows, width)
    parts = 2

    def kernel(left_ref, right_ref, out_ref, held, arrived, sent):
        coming, going = [], []
        for i in range(parts):
            part = pl.ds(i * (count // parts), count // parts)
            for j, ref in enumerate((left_ref, right_ref)):
                to = held.at[part, pl.ds(j * rows, rows)]
                coming.append(pltpu.make_async_copy(ref.at[part], to, arrived.at[2 * i + j]))
            going.append(pltpu.make_async_copy(held.at[part], out_ref.at[part], sent.at[i]))
        for copy in coming:
            copy.start()
        for i in range(parts):
            coming[2 * i].wait()
            coming[2 * i + 1].wait()
            going[i].start()
        for copy in going:
            copy.wait()

    hbm = pl.BlockSpec(memory_space=pltpu.HBM)
    return pl.pallas_call(
        kernel,
        out_shape=jax.ShapeDtypeStruct(shape, BF),
        in_specs=[hbm] * 2,
        out_specs=hbm,
        scratch_shapes=[pltpu.VMEM(shape, BF), pltpu.SemaphoreType.DMA((2 * parts,)), pltpu.SemaphoreType.DMA((parts,))],
        cost_estimate=cost(10**6, 1 << 20),
    )(left, right)


def after_gather(me, whole, right_inverse, left_rows, exact, left_factor, right_factor):
    rows, width = exact.shape
    slab = 128 // rows

    def kernel(me_ref, whole_ref, right_ref, lrows_ref, exact_ref, lf_ref, rf_ref, ln_ref, rn_ref, d_ref, rest, stat):
        me = me_ref[0]
        first = pl.multiple_of((me // slab) * 128, 128)
        mine = pl.multiple_of((me % slab) * rows, rows)
        block = whole_ref[...]
        exact = exact_ref[...]
        my_rows = exact.astype(BF)
        rest[...] = jnp.zeros_like(rest)
        rest[pl.ds(mine, rows), :] = (exact - my_rows.astype(F32)).astype(BF)
        left = mm(lrows_ref[...], block, 1, 0) + mm(lrows_ref[:, pl.ds(first, 128)], rest[...], 1, 0)
        high = left.astype(BF)
        low = (left - high.astype(F32)).astype(BF)
        right = right_ref[...]
        d_ref[0] = (mm(high, right, 1, 0) + mm(low, right, 1, 0)).astype(BF)
        ln_ref[...] = 0.9 * lf_ref[...] + 0.1 * mm(my_rows, block, 1, 1)[None]
        stat[...] = mm(whole_ref[:, pl.ds(first, 128)], block, 0, 0)
        rn_ref[...] = 0.9 * rf_ref[...] + 0.1 * stat[pl.ds(mine, rows), :][None]

    stat_shape = jax.ShapeDtypeStruct((1, rows, width), F32)
    return pl.pallas_call(
        kernel,
        out_shape=(stat_shape, stat_shape, jax.ShapeDtypeStruct((1, rows, width), BF)),
        in_specs=[SMEM] + [VMEM] * 6,
        out_specs=(VMEM, VMEM, VMEM),
        scratch_shapes=[pltpu.VMEM((128, width), BF), pltpu.VMEM((128, width), F32)],
        cost_estimate=cost(10**8, 2 << 20),
    )(me, *(in_vmem(v) for v in (whole, right_inverse, left_rows, exact, left_factor, right_factor)))


def on_device(gradients, owners, left_factor, right_factor, left_root, right_root):
    rows, width = gradients.shape[2:]
    x, z = lax.axis_index("x"), lax.axis_index("z")
    me = lax.axis_index("y") * C + lax.axis_index("c")

    mine = gradients.reshape(Z, X, rows, width)

    def column(step):
        return pick(mine, lax.rem(x + step, X), 1)

    with jax.named_scope("sum_over_x"):
        came = [along_x(column(step).astype(BF), step) for step in (2, 1, 3)]
        over_x = sum((v.astype(F32) for v in came), lax.optimization_barrier(column(0)))
    with jax.named_scope("owner_roots"):
        slots = stacked(left_root.reshape(Y * C, rows, width), right_root.reshape(Y * C, rows, width))
        roots = pick(lax.all_to_all(slots, ROWS, 0, 0, tiled=True), owners[z * X + x], 0)
        over_x, roots = lax.optimization_barrier((over_x.astype(BF), roots))
        right_inverse = lax.all_gather(roots[rows:], ROWS, axis=0, tiled=True)
    with jax.named_scope("sum_over_z"):
        exact = added(lax.all_to_all(over_x, "z", 0, 0, tiled=True))
        my_rows = exact.astype(BF)
    with jax.named_scope("whole_block"):
        my_rows, right_inverse = lax.optimization_barrier((my_rows, right_inverse))
        whole = lax.all_gather(my_rows, ROWS, axis=0, tiled=True)
    with jax.named_scope("direction_and_statistics"):
        return after_gather(me[None], whole, right_inverse, roots[:rows], exact, left_factor, right_factor)


def solution(mesh):
    grid = Mesh(mesh.devices.reshape(Y, C, Z, X), ("y", "c", "z", "x"))
    dp = ("z", "x")
    stat = P(dp, ROWS, None)
    return jax.shard_map(
        on_device,
        mesh=grid,
        in_specs=(P(dp, None, ROWS, None), P(), stat, stat, P(dp, ROWS, None, None), P(dp, ROWS, None, None)),
        out_specs=(stat, stat, stat),
        check_vma=False,
    )
```

```python
import jax
import jax.numpy as jnp
from jax import lax
from jax.experimental import pallas as pl
from jax.experimental.pallas import tpu as pltpu
from jax.sharding import Mesh
from jax.sharding import PartitionSpec as P

Y, C, Z, X = 8, 2, 12, 4
BF, F32 = jnp.bfloat16, jnp.float32
ROWS = ("y", "c")


def along_x(value, step):
    return lax.ppermute(value, "x", [(i, (i + step) % X) for i in range(X)])


def mm(a, b, ca, cb):
    return lax.dot_general(a, b, (((ca,), (cb,)), ((), ())), preferred_element_type=F32)


def pick(array, index, axis):
    return lax.dynamic_index_in_dim(array, index, axis, keepdims=False)


def added(parts):
    total = parts[0].astype(F32)
    for i in range(1, parts.shape[0]):
        total = total + parts[i].astype(F32)
    return total


def in_vmem(value):
    return pltpu.with_memory_space_constraint(value, pltpu.VMEM)


SMEM, VMEM = pl.BlockSpec(memory_space=pltpu.SMEM), pl.BlockSpec(memory_space=pltpu.VMEM)


def cost(flops, size):
    return pl.CostEstimate(flops=flops, bytes_accessed=size, transcendentals=0)


def rows_by_core(core, left, right):
    chips, _, rows, width = left.shape
    shape = (chips, 2 * rows, width)

    def kernel(core_ref, left_ref, right_ref, mine_ref, other_ref, held, arrived, sent):
        core = core_ref[0]
        coming, going = [], []
        for i, (which, out) in enumerate(((1 - core, other_ref), (core, mine_ref))):
            for j, ref in enumerate((left_ref, right_ref)):
                to = held.at[i, :, pl.ds(j * rows, rows)]
                coming.append(pltpu.make_async_copy(ref.at[:, which], to, arrived.at[2 * i + j]))
            going.append(pltpu.make_async_copy(held.at[i], out, sent.at[i]))
        for copy in coming:
            copy.start()
        for i in range(2):
            coming[2 * i].wait()
            coming[2 * i + 1].wait()
            going[i].start()
        for copy in going:
            copy.wait()

    hbm = pl.BlockSpec(memory_space=pltpu.HBM)
    return pl.pallas_call(
        kernel,
        out_shape=(jax.ShapeDtypeStruct(shape, BF),) * 2,
        in_specs=[SMEM, hbm, hbm],
        out_specs=(hbm, hbm),
        scratch_shapes=[pltpu.VMEM((2, *shape), BF), pltpu.SemaphoreType.DMA((4,)), pltpu.SemaphoreType.DMA((2,))],
        cost_estimate=cost(10**6, 1 << 20),
    )(core, left, right)


def of_owner(owners, block, core, mine, other):
    def kernel(owners_ref, block_ref, core_ref, mine_ref, other_ref, out_ref):
        here = lax.rem(owners_ref[block_ref[0]], C) == core_ref[0]

        @pl.when(here)
        def _():
            out_ref[...] = mine_ref[...]

        @pl.when(jnp.logical_not(here))
        def _():
            out_ref[...] = other_ref[...]

    return pl.pallas_call(
        kernel,
        out_shape=jax.ShapeDtypeStruct(mine.shape, BF),
        in_specs=[SMEM] * 3 + [VMEM] * 2,
        out_specs=VMEM,
        cost_estimate=cost(10**6, 1 << 20),
    )(owners, block, core, in_vmem(mine), in_vmem(other))


def first_sum(own, came):
    def kernel(own_ref, came_ref, out_ref):
        for i in range(own_ref.shape[0]):
            out_ref[i] = own_ref[i] + came_ref[i].astype(F32)

    return pl.pallas_call(
        kernel,
        out_shape=jax.ShapeDtypeStruct(own.shape, F32),
        in_specs=[VMEM] * 2,
        out_specs=VMEM,
        cost_estimate=cost(10**11, 2 << 20),
    )(in_vmem(own), in_vmem(came))


def after_gather(me, whole, right_inverse, left_rows, exact, left_factor, right_factor):
    rows, width = exact.shape
    slab = 128 // rows

    def kernel(me_ref, whole_ref, right_ref, lrows_ref, exact_ref, lf_ref, rf_ref, ln_ref, rn_ref, d_ref, rest, stat):
        me = me_ref[0]
        first = pl.multiple_of((me // slab) * 128, 128)
        mine = pl.multiple_of((me % slab) * rows, rows)
        block = whole_ref[...]
        exact = exact_ref[...]
        my_rows = exact.astype(BF)
        rest[...] = jnp.zeros_like(rest)
        rest[pl.ds(mine, rows), :] = (exact - my_rows.astype(F32)).astype(BF)
        left = mm(lrows_ref[...], block, 1, 0) + mm(lrows_ref[:, pl.ds(first, 128)], rest[...], 1, 0)
        high = left.astype(BF)
        low = (left - high.astype(F32)).astype(BF)
        right = right_ref[...]
        d_ref[0] = (mm(high, right, 1, 0) + mm(low, right, 1, 0)).astype(BF)
        ln_ref[...] = 0.9 * lf_ref[...] + 0.1 * mm(my_rows, block, 1, 1)[None]
        stat[...] = mm(whole_ref[:, pl.ds(first, 128)], block, 0, 0)
        rn_ref[...] = 0.9 * rf_ref[...] + 0.1 * stat[pl.ds(mine, rows), :][None]

    stat_shape = jax.ShapeDtypeStruct((1, rows, width), F32)
    return pl.pallas_call(
        kernel,
        out_shape=(stat_shape, stat_shape, jax.ShapeDtypeStruct((1, rows, width), BF)),
        in_specs=[SMEM] + [VMEM] * 6,
        out_specs=(VMEM, VMEM, VMEM),
        scratch_shapes=[pltpu.VMEM((128, width), BF), pltpu.VMEM((128, width), F32)],
        cost_estimate=cost(10**8, 2 << 20),
    )(me, *(in_vmem(v) for v in (whole, right_inverse, left_rows, exact, left_factor, right_factor)))


def on_device(gradients, owners, left_factor, right_factor, left_root, right_root):
    rows, width = gradients.shape[2:]
    x, z = lax.axis_index("x"), lax.axis_index("z")
    me = lax.axis_index("y") * C + lax.axis_index("c")

    mine = gradients.reshape(Z, X, rows, width)

    def column(step, source=mine):
        return pick(source, lax.rem(x + step, X), 1)

    with jax.named_scope("owner_roots"):
        core, block = lax.axis_index("c")[None], z * X + x
        pair = [root.reshape(Y, C, rows, width) for root in (left_root, right_root)]
        keep, give = rows_by_core(core, *pair)
        given = lax.ppermute(give, "c", [(0, 1), (1, 0)])
        given, after_swap, owners_too = lax.optimization_barrier((given, mine, owners))
        slots = of_owner(owners, block[None], core, keep, given)
        spread = lax.all_to_all(slots, "y", 0, 0, tiled=True)
    with jax.named_scope("sum_over_x"):
        across = along_x(column(2).astype(BF), 2)
        beside = [along_x(column(step, after_swap).astype(BF), step) for step in (1, 3)]
        over_x = first_sum(column(0, after_swap), across) + beside[0].astype(F32) + beside[1].astype(F32)
        roots = pick(spread, lax.div(owners_too[block], C), 0)
        over_x, roots = lax.optimization_barrier((over_x.astype(BF), roots))
        right_inverse = lax.all_gather(roots[rows:], ROWS, axis=0, tiled=True)
    with jax.named_scope("sum_over_z"):
        exact = added(lax.all_to_all(over_x, "z", 0, 0, tiled=True))
        my_rows = exact.astype(BF)
    with jax.named_scope("whole_block"):
        my_rows, right_inverse = lax.optimization_barrier((my_rows, right_inverse))
        whole = lax.all_gather(my_rows, ROWS, axis=0, tiled=True)
    with jax.named_scope("direction_and_statistics"):
        return after_gather(me[None], whole, right_inverse, roots[:rows], exact, left_factor, right_factor)


def solution(mesh):
    grid = Mesh(mesh.devices.reshape(Y, C, Z, X), ("y", "c", "z", "x"))
    dp = ("z", "x")
    stat = P(dp, ROWS, None)
    return jax.shard_map(
        on_device,
        mesh=grid,
        in_specs=(P(dp, None, ROWS, None), P(), stat, stat, P(dp, ROWS, None, None), P(dp, ROWS, None, None)),
        out_specs=(stat, stat, stat),
        check_vma=False,
    )
```

```python
import jax
import jax.numpy as jnp
from jax import lax
from jax.experimental import pallas as pl
from jax.experimental.pallas import tpu as pltpu
from jax.sharding import Mesh
from jax.sharding import PartitionSpec as P

Y, C, Z, X = 8, 2, 12, 4
BF, F32 = jnp.bfloat16, jnp.float32
ROWS = ("y", "c")


def along_x(value, step):
    return lax.ppermute(value, "x", [(i, (i + step) % X) for i in range(X)])


def mm(a, b, ca, cb):
    return lax.dot_general(a, b, (((ca,), (cb,)), ((), ())), preferred_element_type=F32)


def pick(array, index, axis):
    return lax.dynamic_index_in_dim(array, index, axis, keepdims=False)


def added(parts):
    total = parts[0].astype(F32)
    for i in range(1, parts.shape[0]):
        total = total + parts[i].astype(F32)
    return total


def in_vmem(value):
    return pltpu.with_memory_space_constraint(value, pltpu.VMEM)


SMEM, VMEM = pl.BlockSpec(memory_space=pltpu.SMEM), pl.BlockSpec(memory_space=pltpu.VMEM)


def cost(flops, size):
    return pl.CostEstimate(flops=flops, bytes_accessed=size, transcendentals=0)


def rows_by_core(core, left, right):
    chips, _, rows, width = left.shape
    shape = (chips, 2 * rows, width)

    def kernel(core_ref, left_ref, right_ref, mine_ref, other_ref, held, arrived, sent):
        core = core_ref[0]
        coming, going = [], []
        for i, (which, out) in enumerate(((1 - core, other_ref), (core, mine_ref))):
            for j, ref in enumerate((left_ref, right_ref)):
                to = held.at[i, :, pl.ds(j * rows, rows)]
                coming.append(pltpu.make_async_copy(ref.at[:, which], to, arrived.at[2 * i + j]))
            going.append(pltpu.make_async_copy(held.at[i], out, sent.at[i]))
        for copy in coming:
            copy.start()
        for i in range(2):
            coming[2 * i].wait()
            coming[2 * i + 1].wait()
            going[i].start()
        for copy in going:
            copy.wait()

    hbm = pl.BlockSpec(memory_space=pltpu.HBM)
    return pl.pallas_call(
        kernel,
        out_shape=(jax.ShapeDtypeStruct(shape, BF),) * 2,
        in_specs=[SMEM, hbm, hbm],
        out_specs=(hbm, hbm),
        scratch_shapes=[pltpu.VMEM((2, *shape), BF), pltpu.SemaphoreType.DMA((4,)), pltpu.SemaphoreType.DMA((2,))],
        cost_estimate=cost(10**6, 1 << 20),
    )(core, left, right)


def of_owner(owners, block, core, mine, other):
    parts = 2
    step = mine.shape[0] // parts

    def kernel(owners_ref, block_ref, core_ref, mine_ref, other_ref, out_ref, held, arrived, sent):
        here = lax.rem(owners_ref[block_ref[0]], C) == core_ref[0]
        pieces = [pl.ds(i * step, step) for i in range(parts)]

        @pl.when(here)
        def _():
            coming = [pltpu.make_async_copy(mine_ref.at[p], held.at[p], arrived.at[i]) for i, p in enumerate(pieces)]
            going = [pltpu.make_async_copy(held.at[p], out_ref.at[p], sent.at[i]) for i, p in enumerate(pieces)]
            for copy in coming:
                copy.start()
            for i in range(parts):
                coming[i].wait()
                going[i].start()
            for copy in going:
                copy.wait()

        @pl.when(jnp.logical_not(here))
        def _():
            copies = [pltpu.make_async_copy(other_ref.at[p], out_ref.at[p], sent.at[i]) for i, p in enumerate(pieces)]
            for copy in copies:
                copy.start()
            for copy in copies:
                copy.wait()

    hbm = pl.BlockSpec(memory_space=pltpu.HBM)
    return pl.pallas_call(
        kernel,
        out_shape=jax.ShapeDtypeStruct(mine.shape, BF),
        in_specs=[SMEM] * 3 + [hbm, VMEM],
        out_specs=hbm,
        scratch_shapes=[pltpu.VMEM(mine.shape, BF), pltpu.SemaphoreType.DMA((parts,)), pltpu.SemaphoreType.DMA((parts,))],
        cost_estimate=cost(10**6, 1 << 20),
    )(owners, block, core, mine, in_vmem(other))


def sum_of(kind, flops, *parts):
    def kernel(*refs):
        *given, out_ref = refs
        for i in range(out_ref.shape[0]):
            out_ref[i] = sum((ref[i].astype(F32) for ref in given[1:]), given[0][i].astype(F32)).astype(kind)

    return pl.pallas_call(
        kernel,
        out_shape=jax.ShapeDtypeStruct(parts[0].shape, kind),
        in_specs=[VMEM] * len(parts),
        out_specs=VMEM,
        cost_estimate=cost(flops, 2 << 20),
    )(parts[0], *(in_vmem(part) for part in parts[1:]))


def after_gather(me, whole, right_inverse, left_rows, exact, left_factor, right_factor):
    rows, width = exact.shape
    slab = 128 // rows

    def kernel(me_ref, whole_ref, right_ref, lrows_ref, exact_ref, lf_ref, rf_ref, ln_ref, rn_ref, d_ref, rest, stat):
        me = me_ref[0]
        first = pl.multiple_of((me // slab) * 128, 128)
        mine = pl.multiple_of((me % slab) * rows, rows)
        block = whole_ref[...]
        exact = exact_ref[...]
        my_rows = exact.astype(BF)
        rest[...] = jnp.zeros_like(rest)
        rest[pl.ds(mine, rows), :] = (exact - my_rows.astype(F32)).astype(BF)
        left = mm(lrows_ref[...], block, 1, 0) + mm(lrows_ref[:, pl.ds(first, 128)], rest[...], 1, 0)
        high = left.astype(BF)
        low = (left - high.astype(F32)).astype(BF)
        right = right_ref[...]
        d_ref[0] = (mm(high, right, 1, 0) + mm(low, right, 1, 0)).astype(BF)
        ln_ref[...] = 0.9 * lf_ref[...] + 0.1 * mm(my_rows, block, 1, 1)[None]
        stat[...] = mm(whole_ref[:, pl.ds(first, 128)], block, 0, 0)
        rn_ref[...] = 0.9 * rf_ref[...] + 0.1 * stat[pl.ds(mine, rows), :][None]

    stat_shape = jax.ShapeDtypeStruct((1, rows, width), F32)
    return pl.pallas_call(
        kernel,
        out_shape=(stat_shape, stat_shape, jax.ShapeDtypeStruct((1, rows, width), BF)),
        in_specs=[SMEM] + [VMEM] * 6,
        out_specs=(VMEM, VMEM, VMEM),
        scratch_shapes=[pltpu.VMEM((128, width), BF), pltpu.VMEM((128, width), F32)],
        cost_estimate=cost(10**8, 2 << 20),
    )(me, *(in_vmem(v) for v in (whole, right_inverse, left_rows, exact, left_factor, right_factor)))


def on_device(gradients, owners, left_factor, right_factor, left_root, right_root):
    rows, width = gradients.shape[2:]
    x, z = lax.axis_index("x"), lax.axis_index("z")
    me = lax.axis_index("y") * C + lax.axis_index("c")

    mine = gradients.reshape(Z, X, rows, width)

    def column(step, source=mine):
        return pick(source, lax.rem(x + step, X), 1)

    with jax.named_scope("owner_roots"):
        core, block = lax.axis_index("c")[None], z * X + x
        pair = [root.reshape(Y, C, rows, width) for root in (left_root, right_root)]
        keep, give = rows_by_core(core, *pair)
        given = lax.ppermute(give, "c", [(0, 1), (1, 0)])
        given, after_swap, owners_too = lax.optimization_barrier((given, mine, owners))
        slots = of_owner(owners, block[None], core, keep, given)
        spread = lax.all_to_all(slots, "y", 0, 0, tiled=True)
    with jax.named_scope("sum_over_x"):
        across = along_x(column(2).astype(BF), 2)
        beside = [along_x(column(step, after_swap).astype(BF), step) for step in (1, 3)]
        over_x = sum_of(F32, 10**11, column(0, after_swap), across)
        over_x = sum_of(BF, 10**6, over_x, *beside)
        roots = pick(spread, lax.div(owners_too[block], C), 0)
        over_x, roots = lax.optimization_barrier((over_x, roots))
        right_inverse = lax.all_gather(roots[rows:], ROWS, axis=0, tiled=True)
    with jax.named_scope("sum_over_z"):
        exact = added(lax.all_to_all(over_x, "z", 0, 0, tiled=True))
        my_rows = exact.astype(BF)
    with jax.named_scope("whole_block"):
        my_rows, right_inverse = lax.optimization_barrier((my_rows, right_inverse))
        whole = lax.all_gather(my_rows, ROWS, axis=0, tiled=True)
    with jax.named_scope("direction_and_statistics"):
        return after_gather(me[None], whole, right_inverse, roots[:rows], exact, left_factor, right_factor)


def solution(mesh):
    grid = Mesh(mesh.devices.reshape(Y, C, Z, X), ("y", "c", "z", "x"))
    dp = ("z", "x")
    stat = P(dp, ROWS, None)
    return jax.shard_map(
        on_device,
        mesh=grid,
        in_specs=(P(dp, None, ROWS, None), P(), stat, stat, P(dp, ROWS, None, None), P(dp, ROWS, None, None)),
        out_specs=(stat, stat, stat),
        check_vma=False,
    )
```

```python
import jax
import jax.numpy as jnp
from jax import lax
from jax.experimental import pallas as pl
from jax.experimental.pallas import tpu as pltpu
from jax.sharding import Mesh
from jax.sharding import PartitionSpec as P

Y, C, Z, X = 8, 2, 12, 4
BF, F32 = jnp.bfloat16, jnp.float32
ROWS = ("y", "c")


def along_x(value, step):
    return lax.ppermute(value, "x", [(i, (i + step) % X) for i in range(X)])


def mm(a, b, ca, cb):
    return lax.dot_general(a, b, (((ca,), (cb,)), ((), ())), preferred_element_type=F32)


def pick(array, index, axis):
    return lax.dynamic_index_in_dim(array, index, axis, keepdims=False)


def added(parts):
    total = parts[0].astype(F32)
    for i in range(1, parts.shape[0]):
        total = total + parts[i].astype(F32)
    return total


def in_vmem(value):
    return pltpu.with_memory_space_constraint(value, pltpu.VMEM)


SMEM, VMEM = pl.BlockSpec(memory_space=pltpu.SMEM), pl.BlockSpec(memory_space=pltpu.VMEM)


def cost(flops, size):
    return pl.CostEstimate(flops=flops, bytes_accessed=size, transcendentals=0)


def rows_by_core(core, left, right):
    chips, _, rows, width = left.shape
    shape = (chips, 2 * rows, width)

    def kernel(core_ref, left_ref, right_ref, mine_ref, other_ref, held, arrived, sent):
        core = core_ref[0]
        coming, going = [], []
        for i, (which, out) in enumerate(((1 - core, other_ref), (core, mine_ref))):
            for j, ref in enumerate((left_ref, right_ref)):
                to = held.at[i, :, pl.ds(j * rows, rows)]
                coming.append(pltpu.make_async_copy(ref.at[:, which], to, arrived.at[2 * i + j]))
            going.append(pltpu.make_async_copy(held.at[i], out, sent.at[i]))
        for copy in coming:
            copy.start()
        for i in range(2):
            coming[2 * i].wait()
            coming[2 * i + 1].wait()
            going[i].start()
        for copy in going:
            copy.wait()

    hbm = pl.BlockSpec(memory_space=pltpu.HBM)
    return pl.pallas_call(
        kernel,
        out_shape=(jax.ShapeDtypeStruct(shape, BF),) * 2,
        in_specs=[SMEM, hbm, hbm],
        out_specs=(hbm, hbm),
        scratch_shapes=[pltpu.VMEM((2, *shape), BF), pltpu.SemaphoreType.DMA((4,)), pltpu.SemaphoreType.DMA((2,))],
        cost_estimate=cost(10**6, 1 << 20),
    )(core, left, right)


def of_owner(owners, block, core, mine, other):
    parts = 2
    step = mine.shape[0] // parts

    def kernel(owners_ref, block_ref, core_ref, mine_ref, other_ref, out_ref, held, arrived, sent):
        here = lax.rem(owners_ref[block_ref[0]], C) == core_ref[0]
        pieces = [pl.ds(i * step, step) for i in range(parts)]

        @pl.when(here)
        def _():
            coming = [pltpu.make_async_copy(mine_ref.at[p], held.at[p], arrived.at[i]) for i, p in enumerate(pieces)]
            going = [pltpu.make_async_copy(held.at[p], out_ref.at[p], sent.at[i]) for i, p in enumerate(pieces)]
            for copy in coming:
                copy.start()
            for i in range(parts):
                coming[i].wait()
                going[i].start()
            for copy in going:
                copy.wait()

        @pl.when(jnp.logical_not(here))
        def _():
            copies = [pltpu.make_async_copy(other_ref.at[p], out_ref.at[p], sent.at[i]) for i, p in enumerate(pieces)]
            for copy in copies:
                copy.start()
            for copy in copies:
                copy.wait()

    hbm = pl.BlockSpec(memory_space=pltpu.HBM)
    return pl.pallas_call(
        kernel,
        out_shape=jax.ShapeDtypeStruct(mine.shape, BF),
        in_specs=[SMEM] * 3 + [hbm, VMEM],
        out_specs=hbm,
        scratch_shapes=[pltpu.VMEM(mine.shape, BF), pltpu.SemaphoreType.DMA((parts,)), pltpu.SemaphoreType.DMA((parts,))],
        cost_estimate=cost(10**6, 1 << 20),
    )(owners, block, core, mine, in_vmem(other))


def sum_of(kind, flops, *parts):
    def kernel(*refs):
        *given, out_ref = refs
        for i in range(out_ref.shape[0]):
            out_ref[i] = sum((ref[i].astype(F32) for ref in given[1:]), given[0][i].astype(F32)).astype(kind)

    return pl.pallas_call(
        kernel,
        out_shape=jax.ShapeDtypeStruct(parts[0].shape, kind),
        in_specs=[VMEM] * len(parts),
        out_specs=VMEM,
        cost_estimate=cost(flops, 2 << 20),
    )(parts[0], *(in_vmem(part) for part in parts[1:]))


def after_gather(me, whole, right_inverse, left_rows, exact, left_factor, right_factor):
    rows, width = exact.shape
    slab = 128 // rows

    def kernel(me_ref, whole_ref, right_ref, lrows_ref, exact_ref, lf_ref, rf_ref, ln_ref, rn_ref, d_ref, rest, stat):
        me = me_ref[0]
        first = pl.multiple_of((me // slab) * 128, 128)
        mine = pl.multiple_of((me % slab) * rows, rows)
        block = whole_ref[...]
        exact = exact_ref[...]
        my_rows = exact.astype(BF)
        rest[...] = jnp.zeros_like(rest)
        rest[pl.ds(mine, rows), :] = (exact - my_rows.astype(F32)).astype(BF)
        left = mm(lrows_ref[...], block, 1, 0) + mm(lrows_ref[:, pl.ds(first, 128)], rest[...], 1, 0)
        high = left.astype(BF)
        low = (left - high.astype(F32)).astype(BF)
        right = right_ref[...]
        d_ref[0] = (mm(high, right, 1, 0) + mm(low, right, 1, 0)).astype(BF)
        ln_ref[...] = 0.9 * lf_ref[...] + 0.1 * mm(my_rows, block, 1, 1)[None]
        stat[...] = mm(whole_ref[:, pl.ds(first, 128)], block, 0, 0)
        rn_ref[...] = 0.9 * rf_ref[...] + 0.1 * stat[pl.ds(mine, rows), :][None]

    stat_shape = jax.ShapeDtypeStruct((1, rows, width), F32)
    return pl.pallas_call(
        kernel,
        out_shape=(stat_shape, stat_shape, jax.ShapeDtypeStruct((1, rows, width), BF)),
        in_specs=[SMEM] + [VMEM] * 6,
        out_specs=(VMEM, VMEM, VMEM),
        scratch_shapes=[pltpu.VMEM((128, width), BF), pltpu.VMEM((128, width), F32)],
        cost_estimate=cost(10**8, 2 << 20),
    )(me, *(in_vmem(v) for v in (whole, right_inverse, left_rows, exact, left_factor, right_factor)))


def on_device(gradients, owners, left_factor, right_factor, left_root, right_root):
    rows, width = gradients.shape[2:]
    x, z = lax.axis_index("x"), lax.axis_index("z")
    me = lax.axis_index("y") * C + lax.axis_index("c")

    mine = gradients.reshape(Z, X, rows, width)

    def column(step, source=mine):
        return pick(source, lax.rem(x + step, X), 1)

    with jax.named_scope("owner_roots"):
        core, block = lax.axis_index("c")[None], z * X + x
        pair = [root.reshape(Y, C, rows, width) for root in (left_root, right_root)]
        keep, give = rows_by_core(core, *pair)
        given = lax.ppermute(give, "c", [(0, 1), (1, 0)])
        given, after_swap, owners_too = lax.optimization_barrier((given, mine, owners))
        slots = of_owner(owners, block[None], core, keep, given)
        spread = lax.all_to_all(slots, "y", 0, 0, tiled=True)
    with jax.named_scope("sum_over_x"):
        across = along_x(column(2).astype(BF), 2)
        beside = [along_x(column(3).astype(BF), 3), along_x(column(1, after_swap).astype(BF), 1)]
        over_x = sum_of(F32, 10**11, column(0, after_swap), across)
        over_x = sum_of(BF, 10**6, over_x, *beside)
        roots = pick(spread, lax.div(owners_too[block], C), 0)
        over_x, roots = lax.optimization_barrier((over_x, roots))
        right_inverse = lax.all_gather(roots[rows:], ROWS, axis=0, tiled=True)
    with jax.named_scope("sum_over_z"):
        exact = added(lax.all_to_all(over_x, "z", 0, 0, tiled=True))
        my_rows = exact.astype(BF)
    with jax.named_scope("whole_block"):
        my_rows, right_inverse = lax.optimization_barrier((my_rows, right_inverse))
        whole = lax.all_gather(my_rows, ROWS, axis=0, tiled=True)
    with jax.named_scope("direction_and_statistics"):
        return after_gather(me[None], whole, right_inverse, roots[:rows], exact, left_factor, right_factor)


def solution(mesh):
    grid = Mesh(mesh.devices.reshape(Y, C, Z, X), ("y", "c", "z", "x"))
    dp = ("z", "x")
    stat = P(dp, ROWS, None)
    return jax.shard_map(
        on_device,
        mesh=grid,
        in_specs=(P(dp, None, ROWS, None), P(), stat, stat, P(dp, ROWS, None, None), P(dp, ROWS, None, None)),
        out_specs=(stat, stat, stat),
        check_vma=False,
    )
```
